512 devices in a mesh: rep: 64 (over z_lo, y, x), fsdp: 8 (over z_hi, core).
Axes of the slice: x: 4, y: 8, z: 8 (z_hi: 4, z_lo: 2; z = z_hi * 2 + z_lo), core: 2. Of those that a mesh axis runs over, the one named last changes fastest.
Arguments:
- inner_weights: float32 [64, 256, 4608], P('rep', 'fsdp'), may hold values from -16 to 16
- grads: bfloat16 [64, 256, 4608], P('rep', 'fsdp'), may hold values from -6000 to 6000
- first_moment: float32 [64, 256, 4608], P('rep', 'fsdp'), may hold values from -1.5 to 1.5
- second_moment: float32 [64, 256, 4608], P('rep', 'fsdp'), may hold values from 0.001 to 0.05
- anchor: float32 [256, 4608], P('fsdp', 'rep'), may hold values from -6 to 6
- outer_momentum: float32 [256, 4608], P('fsdp', 'rep'), may hold values from -4 to 4
Outputs:
- new_params: float32 [256, 4608], P('fsdp')
- new_momentum: float32 [256, 4608], P('fsdp', 'rep')
- new_first: float32 [64, 256, 4608], P('rep', 'fsdp')
- new_second: float32 [64, 256, 4608], P('rep', 'fsdp')
The draws below stay inside these ranges and needn't reach their ends.
All inputs are finite; a program needn't handle non-finite values.
Results may differ from the reference program's by a relative error of at most 0.0018.
Values sent between devices are 32-bit elements; how exact they have to be, the bound alone decides.
No kernel may reach another device: no remote copies, remote signals or barrier semaphores. Data moves between devices by JAX's collectives and lax.ppermute only.
A program may use at most 64 MiB of HBM per device.

```python
import math
import jax
import jax.numpy as jnp
from jax import lax

D = 4608
ROWS_DEV = 32
ROWS = 256
N_REP = 64
N_FSDP = 8


def draw_grads(key, part):
    key = jax.random.fold_in(key, 7)
    key_base = jax.random.fold_in(key, 0)
    key_rows = jax.random.fold_in(key, 1)
    key_cols = jax.random.fold_in(key, 2)
    key_order = jax.random.fold_in(key, 4)
    key_offset = jax.random.fold_in(key, 5)
    total_rows = N_FSDP * ROWS_DEV
    shape = (N_REP, total_rows, D)
    base = jnp.clip(jax.random.normal(key_base, shape, jnp.float32), -6.0, 6.0)
    row_scale = jnp.exp(jax.random.uniform(key_rows, (N_REP, total_rows, 1), jnp.float32) * math.log(10.0))
    col_scale = jnp.exp(jax.random.uniform(key_cols, (1, 1, D), jnp.float32) * math.log(10.0))
    order = jax.random.permutation(key_order, N_REP).astype(jnp.float32)
    offset = jax.random.uniform(key_offset, (N_REP,), jnp.float32)
    replica_scale = jnp.exp(-3.0 * math.log(10.0) * (order + offset) / N_REP)
    shard = (jnp.arange(total_rows) // ROWS_DEV).astype(jnp.float32)
    ramp = 1.0 + 2.0 * shard / max(N_FSDP - 1, 1)
    return (base * row_scale * col_scale * ramp[None, :, None] * replica_scale[:, None, None]).astype(jnp.bfloat16)


def spiked(result, rng, source, target, blocks, factor):
    owner, partner = [(jnp.arange(result.shape[position]) // (result.shape[position] // blocks)).reshape([-1 if axis == position else 1 for axis in range(result.ndim)]) for position in (source, target)]
    chosen = jax.random.permutation(rng, blocks)[partner]
    strong = (owner == chosen) | (owner == (partner + blocks // 2) % blocks)
    return jnp.where(strong, factor * result, result)


def shard_levels(key, dims, shards, low, high):
    def one(axis_at, blocks):
        steps = jax.random.uniform(jax.random.fold_in(jax.random.fold_in(key, 6), axis_at), (blocks,), jnp.float32, low / len(shards), high / len(shards))
        return jnp.repeat(jnp.exp(steps), dims[axis_at] // blocks).reshape((-1,) + (1,) * (len(dims) - axis_at - 1))

    factor_of = one(*shards[0])
    for cut in shards[1:]:
        factor_of = factor_of * one(*cut)
    return factor_of


def normal_values(own_key, extent, spread, bound, shards=(), dtype=jnp.bfloat16):
    values = spread * jax.random.normal(own_key, extent, jnp.float32)
    if shards:
        values = values * shard_levels(own_key, extent, shards, -0.22, 0.18)
    return jnp.clip(values, -bound, bound).astype(dtype)


def noise_with(rng, extent, spread, most, cuts, heavy, held_as=jnp.bfloat16):
    array = spread * jax.random.normal(rng, extent, jnp.float32)
    if cuts:
        array = array * shard_levels(rng, extent, cuts, -0.22, 0.18)
    return jnp.clip(spiked(array, jax.random.fold_in(rng, 3), *heavy), -most, most).astype(held_as)


def setup_inputs(seed: int = 0) -> dict:
    streams_of = jax.random.split(jax.random.key(seed), 7)
    return {
        "inner_weights": noise_with(streams_of[0], (N_REP, ROWS, D), 1.0, 16.0, ((0, 64), (1, 8)), (0, 2, 64, 4.0), jnp.float32),
        "grads": draw_grads(jax.random.fold_in(streams_of[6], 71), 0),
        "first_moment": normal_values(streams_of[2], (N_REP, ROWS, D), 0.1, 1.5, ((0, 64), (1, 8)), jnp.float32),
        "second_moment": jnp.clip(jnp.exp(math.log(0.05) - 3.912023 * jax.random.uniform(streams_of[3], (N_REP, ROWS, D), jnp.float32) ** shard_levels(streams_of[3], (N_REP, ROWS, D), ((0, 64), (1, 8)), -0.2, 0.2)), 0.001, 0.05),
        "anchor": normal_values(streams_of[4], (ROWS, D), 1.0, 6.0, ((0, 8), (1, 64)), jnp.float32),
        "outer_momentum": normal_values(streams_of[5], (ROWS, D), 0.3, 4.0, ((0, 8), (1, 64)), jnp.float32),
    }


beta_one = 0.9
beta_two = 0.95
inner_rate = 0.01
weight_decay = 0.1
adam_eps = 1e-08
clip_rms = 0.5
outer_rate = 0.7
outer_beta = 0.9

def reference(inner_weights, grads, first_moment, second_moment, anchor, outer_momentum):
    gradient = grads.astype(jnp.float32)
    norm_square = lax.optimization_barrier(jnp.sum(gradient * gradient, axis=(1, 2)))
    entries = ROWS * D
    clip_factor = jnp.minimum(1.0, clip_rms * math.sqrt(entries) / jnp.sqrt(norm_square + 1e-06))
    clipped = gradient * clip_factor[:, None, None]
    new_first = beta_one * first_moment + (1.0 - beta_one) * clipped
    new_second = beta_two * second_moment + (1.0 - beta_two) * clipped * clipped
    stepped = inner_weights - inner_rate * (new_first / (jnp.sqrt(new_second) + adam_eps) + weight_decay * inner_weights)
    change = anchor - lax.optimization_barrier(jnp.sum(stepped, axis=0)) / N_REP
    new_momentum = outer_beta * outer_momentum + change
    new_params = anchor - outer_rate * (change + outer_beta * new_momentum)
    return (new_params, new_momentum, new_first, new_second)
```

```python
import math

import jax
import jax.numpy as jnp
from jax import lax
from jax.sharding import Mesh
from jax.sharding import PartitionSpec as P

beta_one = 0.9
beta_two = 0.95
inner_rate = 0.01
weight_decay = 0.1
adam_eps = 1e-08
clip_rms = 0.5
outer_rate = 0.7
outer_beta = 0.9

FSDP = ("fz", "fc")
NEAR = ("zl", "x", "yl")
FAR = ("yh",)
REP = ("zl", "yh", "yl", "x")

gain = outer_rate * (1.0 + outer_beta)
keep = 1.0 - gain
drag = outer_rate * outer_beta * outer_beta


def exchange(value, axes):
    return lax.all_to_all(value, axes, 0, 0, tiled=True)


def spread(value, n):
    return jnp.broadcast_to(value[None], (n,) + value.shape)


def body(inner_weights, grads, first_moment, second_moment, anchor, outer_momentum):
    rows, width = grads.shape[1:]
    shards = lax.axis_size(FSDP)
    replicas = lax.axis_size(REP)
    near = lax.axis_size(NEAR)
    far = lax.axis_size(FAR)
    columns = anchor.shape[1]
    first_column = lax.axis_index(REP) * columns

    gradient = grads[0].astype(jnp.float32)
    partial_sum = jnp.sum(gradient * gradient)
    norm_square = jnp.sum(exchange(jnp.broadcast_to(partial_sum, (shards, 128)), FSDP)[:, 0])
    entries = rows * width * shards
    clip_factor = jnp.minimum(1.0, clip_rms * math.sqrt(entries) / jnp.sqrt(norm_square + 1e-06))
    clipped = gradient * clip_factor
    new_first = beta_one * first_moment[0] + (1.0 - beta_one) * clipped
    new_second = beta_two * second_moment[0] + (1.0 - beta_two) * clipped * clipped
    stepped = inner_weights[0] - inner_rate * (
        new_first / (jnp.sqrt(new_second) + adam_eps) + weight_decay * inner_weights[0]
    )
    part = (gain / replicas) * stepped
    own = lax.dynamic_slice_in_dim(part, first_column, columns, 1)
    part = lax.dynamic_update_slice_in_dim(
        part, own + keep * anchor - drag * outer_momentum, first_column, 1
    )
    groups = rows // 8
    cuts = near // groups
    blocks = part.reshape(groups, 8, cuts, width // cuts).transpose(0, 2, 1, 3)
    blocks = blocks.reshape(near, 8, width // cuts)
    mine = jnp.sum(exchange(blocks, NEAR), axis=0)
    mine = jnp.sum(exchange(spread(mine, far), FAR), axis=0)
    full = exchange(spread(mine, near), NEAR)
    new_params = full.reshape(groups, cuts, 8, width // cuts).transpose(0, 2, 1, 3).reshape(rows, width)
    own = lax.dynamic_slice_in_dim(new_params, first_column, columns, 1)
    mean = (own - keep * anchor + drag * outer_momentum) / gain
    new_momentum = outer_beta * outer_momentum + (anchor - mean)
    return (new_params, new_momentum, new_first[None], new_second[None])


def solution(mesh):
    fine = Mesh(
        mesh.devices.reshape(2, 4, 2, 4, 4, 2), ("zl", "yh", "yl", "x", "fz", "fc")
    )
    placed = (
        P(REP, FSDP, None),
        P(REP, FSDP, None),
        P(REP, FSDP, None),
        P(REP, FSDP, None),
        P(FSDP, REP),
        P(FSDP, REP),
    )
    return jax.shard_map(
        body,
        mesh=fine,
        in_specs=placed,
        out_specs=(
            P(FSDP, None),
            P(FSDP, REP),
            P(REP, FSDP, None),
            P(REP, FSDP, None),
        ),
        check_vma=False,
    )
```

```python
import math

import jax
import jax.numpy as jnp
from jax import lax
from jax.experimental import pallas as pl
from jax.experimental.pallas import tpu as pltpu
from jax.sharding import Mesh
from jax.sharding import PartitionSpec as P

beta_one = 0.9
beta_two = 0.95
inner_rate = 0.01
weight_decay = 0.1
adam_eps = 1e-08
clip_rms = 0.5
outer_rate = 0.7
outer_beta = 0.9

FSDP = ("fz", "fc")
NEAR = ("zl", "x", "yl")
FAR = ("yh",)
REP = ("zl", "yh", "yl", "x")

gain = outer_rate * (1.0 + outer_beta)
keep = 1.0 - gain
drag = outer_rate * outer_beta * outer_beta

SUB, LANE = 8, 128
PIECES = 2
SMALL = pltpu.CompilerParams(vmem_limit_bytes=4 * 2**20)
VMEM = pl.BlockSpec(memory_space=pltpu.VMEM)
ANY = pl.BlockSpec(memory_space=pl.ANY)
f32 = jnp.float32


def exchange(value, axes):
    return lax.all_to_all(value, axes, 0, 0, tiled=True)


def in_hbm(value):
    return pltpu.with_memory_space_constraint(value, pltpu.HBM)


def square_kernel(grads_ref, parts_ref, held_ref, arrived):
    rows, width = grads_ref.shape[1:]
    step = rows // PIECES
    copies = []
    for i in range(PIECES):
        here = (0, slice(i * step, (i + 1) * step))
        copies.append(pltpu.make_async_copy(grads_ref.at[here], held_ref.at[here], arrived.at[i]))
        copies[-1].start()
    total = jnp.zeros((step, LANE), f32)
    for i in range(PIECES):
        copies[i].wait()
        for at in range(0, width, LANE):
            tile = held_ref[0, i * step : (i + 1) * step, at : at + LANE].astype(f32)
            total += tile * tile
    tile = sum(total[at : at + SUB] for at in range(0, step, SUB))
    parts_ref[...] = jnp.broadcast_to(tile[None], parts_ref.shape)


def first_column(columns):
    index = 0
    for axis in REP:
        index = index * lax.axis_size(axis) + lax.axis_index(axis)
    return index * columns


def window(first, width):
    tile = jnp.minimum(first // LANE, width // LANE - 2)
    start = pl.multiple_of(tile * LANE, LANE)
    return start, first - start


def hold_kernel(
    scale, weights_ref, first_ref, second_ref, anchor_ref, outer_ref, base_ref, old_first_ref, old_second_ref, arrived
):
    copies = []
    pairs = ((weights_ref, base_ref), (first_ref, old_first_ref), (second_ref, old_second_ref))
    for i, (given, held) in enumerate(pairs):
        copies.append(pltpu.make_async_copy(given, held, arrived.at[i]))
        copies[-1].start()
    rows, width = base_ref.shape[1:]
    mine = keep * anchor_ref[...] - drag * outer_ref[...]
    columns = mine.shape[1]
    start, shift = window(first_column(columns), width)
    mine = jnp.concatenate([mine, jnp.zeros((rows, 2 * LANE - columns), f32)], axis=1)
    mine = pltpu.roll(mine, shift, 1)
    copies[0].wait()
    base_ref[...] = (scale * (1.0 - inner_rate * weight_decay)) * base_ref[...]
    base_ref[0, :, pl.ds(start, 2 * LANE)] += mine
    copies[1].wait()
    old_first_ref[...] = beta_one * old_first_ref[...]
    copies[2].wait()
    old_second_ref[...] = beta_two * old_second_ref[...]


def step_kernel(
    scale, entries, parts_ref, grads_ref, base_ref, old_first_ref, old_second_ref, blocks_ref, new_first_ref, new_second_ref
):
    rows, width = base_ref.shape[1:]
    cut = blocks_ref.shape[2]
    cuts = width // cut
    norm_square = jnp.sum(parts_ref[...])
    clip_factor = jnp.minimum(
        1.0, clip_rms * math.sqrt(entries) * lax.rsqrt(jnp.full((SUB, LANE), norm_square + 1e-06))
    )
    clip_row = clip_factor[:1, :1]
    for top in range(0, rows, 2 * SUB):
        for at in range(cuts):
            here = (0, slice(top, top + 2 * SUB), slice(at * cut, (at + 1) * cut))
            clipped = grads_ref[here].astype(f32) * clip_row
            new_first = old_first_ref[here] + (1.0 - beta_one) * clipped
            new_second = old_second_ref[here] + (1.0 - beta_two) * clipped * clipped
            new_first_ref[here] = new_first
            new_second_ref[here] = new_second
            block = base_ref[here] - (scale * inner_rate) * (new_first / (jnp.sqrt(new_second) + adam_eps))
            for half in range(2):
                blocks_ref[(top // SUB + half) * cuts + at] = block[half * SUB : (half + 1) * SUB]


def sum_kernel(given_ref, sums_ref):
    total = given_ref[0]
    for at in range(1, given_ref.shape[0]):
        total += given_ref[at]
    sums_ref[...] = jnp.broadcast_to(total[None], sums_ref.shape)


def sum_spread(given, n):
    return pl.pallas_call(
        sum_kernel,
        out_shape=pltpu.VMEM((n,) + given.shape[1:], f32),
        in_specs=[VMEM],
        out_specs=VMEM,
        compiler_params=SMALL,
        name="sum",
    )(given)


def copies_kernel(given_ref, out_ref, total_ref, done):
    total = given_ref[0]
    for at in range(1, given_ref.shape[0]):
        total += given_ref[at]
    total_ref[...] = total
    copies = [pltpu.make_async_copy(total_ref, out_ref.at[at], done.at[at]) for at in range(out_ref.shape[0])]
    for copy in copies:
        copy.start()
    for copy in copies:
        copy.wait()


def sum_copies(given, n):
    return pl.pallas_call(
        copies_kernel,
        out_shape=jax.ShapeDtypeStruct((n,) + given.shape[1:], f32),
        in_specs=[VMEM],
        out_specs=ANY,
        scratch_shapes=[pltpu.VMEM(given.shape[1:], f32), pltpu.SemaphoreType.DMA((n,))],
        compiler_params=SMALL,
        name="copies",
    )(given)


def outer_kernel(full_ref, anchor_ref, outer_ref, params_ref, momentum_ref, own_ref, done):
    copies = []
    for at in range(full_ref.shape[0] // SUB):
        here = slice(at * SUB, (at + 1) * SUB)
        copies.append(pltpu.make_async_copy(full_ref.at[here], params_ref.at[here], done.at[at]))
        copies[-1].start()
    columns = anchor_ref.shape[1]
    start, shift = window(first_column(columns), full_ref.shape[1])
    near = full_ref[:, pl.ds(start, 2 * LANE)]
    own = pltpu.roll(near, 2 * LANE - shift, 1)[:, :columns]
    mean = (own - keep * anchor_ref[...] + drag * outer_ref[...]) / gain
    own_ref[...] = outer_beta * outer_ref[...] + (anchor_ref[...] - mean)
    copies.append(pltpu.make_async_copy(own_ref, momentum_ref, done.at[len(copies)]))
    copies[-1].start()
    for copy in copies:
        copy.wait()


def body(inner_weights, grads, first_moment, second_moment, anchor, outer_momentum):
    rows, width = grads.shape[1:]
    shards = lax.axis_size(FSDP)
    replicas = lax.axis_size(REP)
    near = lax.axis_size(NEAR)
    far = lax.axis_size(FAR)
    columns = anchor.shape[1]
    groups = rows // SUB
    cuts = near // groups
    scale = gain / replicas

    parts, grads = pl.pallas_call(
        square_kernel,
        out_shape=(pltpu.VMEM((shards, SUB, LANE), f32), pltpu.VMEM(grads.shape, grads.dtype)),
        in_specs=[ANY],
        out_specs=(VMEM, VMEM),
        scratch_shapes=[pltpu.SemaphoreType.DMA((PIECES,))],
        compiler_params=SMALL,
        name="square",
    )(in_hbm(grads))
    parts = exchange(parts, FSDP)

    def hold(*refs):
        hold_kernel(scale, *refs)

    held = pl.pallas_call(
        hold,
        out_shape=(pltpu.VMEM((1, rows, width), f32),) * 3,
        in_specs=[ANY, ANY, ANY, VMEM, VMEM],
        out_specs=(VMEM,) * 3,
        scratch_shapes=[pltpu.SemaphoreType.DMA((3,))],
        compiler_params=SMALL,
        cost_estimate=pl.CostEstimate(flops=10**7, bytes_accessed=10**7, transcendentals=0),
        name="hold",
    )(in_hbm(inner_weights), in_hbm(first_moment), in_hbm(second_moment), anchor, outer_momentum)

    def step(*refs):
        step_kernel(scale, rows * width * shards, *refs)

    blocks, new_first, new_second = pl.pallas_call(
        step,
        out_shape=(
            pltpu.VMEM((near, SUB, width // cuts), f32),
            pltpu.VMEM((1, rows, width), f32),
            pltpu.VMEM((1, rows, width), f32),
        ),
        in_specs=[VMEM] * 5,
        out_specs=(VMEM,) * 3,
        input_output_aliases={3: 1, 4: 2},
        compiler_params=SMALL,
        name="step",
    )(parts, grads, *held)
    mine = sum_spread(exchange(blocks, NEAR), far)
    mine = sum_copies(exchange(mine, FAR), near)
    full = exchange(mine, NEAR)
    full = full.reshape(groups, cuts, SUB, width // cuts).transpose(0, 2, 1, 3).reshape(rows, width)
    new_params, new_momentum = pl.pallas_call(
        outer_kernel,
        out_shape=(jax.ShapeDtypeStruct((rows, width), f32), jax.ShapeDtypeStruct((rows, columns), f32)),
        in_specs=[VMEM] * 3,
        out_specs=(ANY, ANY),
        scratch_shapes=[pltpu.VMEM((rows, columns), f32), pltpu.SemaphoreType.DMA((groups + 1,))],
        compiler_params=SMALL,
        name="outer",
    )(full, anchor, outer_momentum)
    return (new_params, new_momentum, new_first, new_second)


def solution(mesh):
    fine = Mesh(
        mesh.devices.reshape(2, 4, 2, 4, 4, 2), ("zl", "yh", "yl", "x", "fz", "fc")
    )
    placed = (
        P(REP, FSDP, None),
        P(REP, FSDP, None),
        P(REP, FSDP, None),
        P(REP, FSDP, None),
        P(FSDP, REP),
        P(FSDP, REP),
    )
    return jax.shard_map(
        body,
        mesh=fine,
        in_specs=placed,
        out_specs=(
            P(FSDP, None),
            P(FSDP, REP),
            P(REP, FSDP, None),
            P(REP, FSDP, None),
        ),
        check_vma=False,
    )
```

```python
import math

import jax
import jax.numpy as jnp
from jax import lax
from jax.experimental import pallas as pl
from jax.experimental.pallas import tpu as pltpu
from jax.sharding import Mesh
from jax.sharding import PartitionSpec as P

beta_one = 0.9
beta_two = 0.95
inner_rate = 0.01
weight_decay = 0.1
adam_eps = 1e-08
clip_rms = 0.5
outer_rate = 0.7
outer_beta = 0.9

FSDP = ("fz", "fc")
NEAR = ("zl", "x", "yl")
FAR = ("yh",)
REP = ("zl", "yh", "yl", "x")

gain = outer_rate * (1.0 + outer_beta)
keep = 1.0 - gain
drag = outer_rate * outer_beta * outer_beta

SUB, LANE = 8, 128
PIECES = 4
SMALL = pltpu.CompilerParams(vmem_limit_bytes=4 * 2**20)
VMEM = pl.BlockSpec(memory_space=pltpu.VMEM)
ANY = pl.BlockSpec(memory_space=pl.ANY)
f32 = jnp.float32


def exchange(value, axes):
    return lax.all_to_all(value, axes, 0, 0, tiled=True)


def in_hbm(value):
    return pltpu.with_memory_space_constraint(value, pltpu.HBM)


def square_kernel(grads_ref, parts_ref, held_ref, arrived):
    rows, width = grads_ref.shape[1:]
    step = 2 * SUB
    cut = width // PIECES
    pieces = [(top, at) for top in range(0, rows, step) for at in range(0, width, cut)]
    copies = []
    for i, (top, at) in enumerate(pieces):
        here = (0, slice(top, top + step), slice(at, at + cut))
        copies.append(pltpu.make_async_copy(grads_ref.at[here], held_ref.at[here], arrived.at[i]))
        copies[-1].start()
    total = jnp.zeros((step, LANE), f32)
    for copy, (top, at) in zip(copies, pieces):
        copy.wait()
        for lane in range(at, at + cut, LANE):
            tile = held_ref[0, top : top + step, lane : lane + LANE].astype(f32)
            total += tile * tile
    tile = total[:SUB] + total[SUB:]
    parts_ref[...] = jnp.broadcast_to(tile[None], parts_ref.shape)


def first_column(columns):
    index = 0
    for axis in REP:
        index = index * lax.axis_size(axis) + lax.axis_index(axis)
    return index * columns


def window(first, width):
    tile = jnp.minimum(first // LANE, width // LANE - 2)
    start = pl.multiple_of(tile * LANE, LANE)
    return start, first - start


def hold_kernel(
    scale, weights_ref, first_ref, second_ref, anchor_ref, outer_ref, base_ref, old_first_ref, old_second_ref, arrived
):
    copies = []
    pairs = ((weights_ref, base_ref), (first_ref, old_first_ref), (second_ref, old_second_ref))
    for i, (given, held) in enumerate(pairs):
        copies.append(pltpu.make_async_copy(given, held, arrived.at[i]))
        copies[-1].start()
    rows, width = base_ref.shape[1:]
    mine = keep * anchor_ref[...] - drag * outer_ref[...]
    columns = mine.shape[1]
    start, shift = window(first_column(columns), width)
    mine = jnp.concatenate([mine, jnp.zeros((rows, 2 * LANE - columns), f32)], axis=1)
    mine = pltpu.roll(mine, shift, 1)
    copies[0].wait()
    base_ref[...] = (scale * (1.0 - inner_rate * weight_decay)) * base_ref[...]
    base_ref[0, :, pl.ds(start, 2 * LANE)] += mine
    copies[1].wait()
    old_first_ref[...] = beta_one * old_first_ref[...]
    copies[2].wait()
    old_second_ref[...] = beta_two * old_second_ref[...]


def step_kernel(
    scale, entries, parts_ref, grads_ref, base_ref, old_first_ref, old_second_ref, blocks_ref, new_first_ref, new_second_ref
):
    rows, width = base_ref.shape[1:]
    cut = blocks_ref.shape[2]
    cuts = width // cut
    norm_square = jnp.sum(parts_ref[...])
    clip_factor = jnp.minimum(
        1.0, clip_rms * math.sqrt(entries) * lax.rsqrt(jnp.full((SUB, LANE), norm_square + 1e-06))
    )
    clip_row = clip_factor[:1, :1]
    for top in range(0, rows, 2 * SUB):
        for at in range(cuts):
            here = (0, slice(top, top + 2 * SUB), slice(at * cut, (at + 1) * cut))
            clipped = grads_ref[here].astype(f32) * clip_row
            new_first = old_first_ref[here] + (1.0 - beta_one) * clipped
            new_second = old_second_ref[here] + (1.0 - beta_two) * clipped * clipped
            new_first_ref[here] = new_first
            new_second_ref[here] = new_second
            block = base_ref[here] - (scale * inner_rate) * (new_first / (jnp.sqrt(new_second) + adam_eps))
            for half in range(2):
                blocks_ref[(top // SUB + half) * cuts + at] = block[half * SUB : (half + 1) * SUB]


def sum_kernel(given_ref, *refs):
    sums_ref = refs[-1]
    total = given_ref[0]
    for at in range(1, given_ref.shape[0]):
        total += given_ref[at]
    sums_ref[...] = jnp.broadcast_to(total[None], sums_ref.shape)


def sum_spread(given, n, *after):
    return pl.pallas_call(
        sum_kernel,
        out_shape=pltpu.VMEM((n,) + given.shape[1:], f32),
        in_specs=[VMEM] * (1 + len(after)),
        out_specs=VMEM,
        compiler_params=SMALL,
        name="sum",
    )(given, *after)


def copies_kernel(given_ref, *refs):
    out_ref, total_ref, done = refs[-3:]
    total = given_ref[0]
    for at in range(1, given_ref.shape[0]):
        total += given_ref[at]
    total_ref[...] = total
    copies = [pltpu.make_async_copy(total_ref, out_ref.at[at], done.at[at]) for at in range(out_ref.shape[0])]
    for copy in copies:
        copy.start()
    for copy in copies:
        copy.wait()


def sum_copies(given, n):
    return pl.pallas_call(
        copies_kernel,
        out_shape=jax.ShapeDtypeStruct((n,) + given.shape[1:], f32),
        in_specs=[VMEM],
        out_specs=ANY,
        scratch_shapes=[pltpu.VMEM(given.shape[1:], f32), pltpu.SemaphoreType.DMA((n,))],
        compiler_params=SMALL,
        name="copies",
    )(given)


def write_kernel(first_ref, second_ref, _after, new_first_ref, new_second_ref, mark_ref, done):
    copies = []
    for given, out in ((first_ref, new_first_ref), (second_ref, new_second_ref)):
        for at in range(0, given.shape[1], SUB):
            here = (0, slice(at, at + SUB))
            copies.append(pltpu.make_async_copy(given.at[here], out.at[here], done.at[len(copies)]))
            copies[-1].start()
    mark_ref[...] = jnp.zeros(mark_ref.shape, f32)
    for copy in copies:
        copy.wait()


def write_moments(first, second, after):
    return pl.pallas_call(
        write_kernel,
        out_shape=(jax.ShapeDtypeStruct(first.shape, f32),) * 2 + (pltpu.VMEM((SUB, LANE), f32),),
        in_specs=[VMEM, VMEM, ANY],
        out_specs=(ANY, ANY, VMEM),
        scratch_shapes=[pltpu.SemaphoreType.DMA((2 * first.shape[1] // SUB,))],
        compiler_params=SMALL,
        cost_estimate=pl.CostEstimate(flops=10**6, bytes_accessed=4 * 10**6, transcendentals=0),
        name="write",
    )(first, second, after)


def outer_kernel(full_ref, anchor_ref, outer_ref, params_ref, momentum_ref, own_ref, done):
    copies = []
    for at in range(full_ref.shape[0] // SUB):
        here = slice(at * SUB, (at + 1) * SUB)
        copies.append(pltpu.make_async_copy(full_ref.at[here], params_ref.at[here], done.at[at]))
        copies[-1].start()
    columns = anchor_ref.shape[1]
    start, shift = window(first_column(columns), full_ref.shape[1])
    near = full_ref[:, pl.ds(start, 2 * LANE)]
    own = pltpu.roll(near, 2 * LANE - shift, 1)[:, :columns]
    mean = (own - keep * anchor_ref[...] + drag * outer_ref[...]) / gain
    own_ref[...] = outer_beta * outer_ref[...] + (anchor_ref[...] - mean)
    copies.append(pltpu.make_async_copy(own_ref, momentum_ref, done.at[len(copies)]))
    copies[-1].start()
    for copy in copies:
        copy.wait()


def body(inner_weights, grads, first_moment, second_moment, anchor, outer_momentum):
    rows, width = grads.shape[1:]
    shards = lax.axis_size(FSDP)
    replicas = lax.axis_size(REP)
    near = lax.axis_size(NEAR)
    far = lax.axis_size(FAR)
    columns = anchor.shape[1]
    groups = rows // SUB
    cuts = near // groups
    scale = gain / replicas

    parts, grads = pl.pallas_call(
        square_kernel,
        out_shape=(pltpu.VMEM((shards, SUB, LANE), f32), pltpu.VMEM(grads.shape, grads.dtype)),
        in_specs=[ANY],
        out_specs=(VMEM, VMEM),
        scratch_shapes=[pltpu.SemaphoreType.DMA((rows // (2 * SUB) * PIECES,))],
        compiler_params=SMALL,
        name="square",
    )(in_hbm(grads))
    parts = exchange(parts, FSDP)

    def hold(*refs):
        hold_kernel(scale, *refs)

    held = pl.pallas_call(
        hold,
        out_shape=(pltpu.VMEM((1, rows, width), f32),) * 3,
        in_specs=[ANY, ANY, ANY, VMEM, VMEM],
        out_specs=(VMEM,) * 3,
        scratch_shapes=[pltpu.SemaphoreType.DMA((3,))],
        compiler_params=SMALL,
        cost_estimate=pl.CostEstimate(flops=10**7, bytes_accessed=10**7, transcendentals=0),
        name="hold",
    )(in_hbm(inner_weights), in_hbm(first_moment), in_hbm(second_moment), anchor, outer_momentum)

    def step(*refs):
        step_kernel(scale, rows * width * shards, *refs)

    blocks, new_first, new_second = pl.pallas_call(
        step,
        out_shape=(
            pltpu.VMEM((near, SUB, width // cuts), f32),
            pltpu.VMEM((1, rows, width), f32),
            pltpu.VMEM((1, rows, width), f32),
        ),
        in_specs=[VMEM] * 5,
        out_specs=(VMEM,) * 3,
        input_output_aliases={3: 1, 4: 2},
        compiler_params=SMALL,
        name="step",
    )(parts, grads, *held)
    mine = sum_copies(exchange(blocks, NEAR), far)
    new_first, new_second, mark = write_moments(new_first, new_second, mine)
    mine = sum_spread(exchange(mine, FAR), near, mark)
    full = exchange(mine, NEAR)
    full = full.reshape(groups, cuts, SUB, width // cuts).transpose(0, 2, 1, 3).reshape(rows, width)
    new_params, new_momentum = pl.pallas_call(
        outer_kernel,
        out_shape=(jax.ShapeDtypeStruct((rows, width), f32), jax.ShapeDtypeStruct((rows, columns), f32)),
        in_specs=[VMEM] * 3,
        out_specs=(ANY, ANY),
        scratch_shapes=[pltpu.VMEM((rows, columns), f32), pltpu.SemaphoreType.DMA((groups + 1,))],
        compiler_params=SMALL,
        name="outer",
    )(full, anchor, outer_momentum)
    return (new_params, new_momentum, new_first, new_second)


def solution(mesh):
    fine = Mesh(
        mesh.devices.reshape(2, 4, 2, 4, 4, 2), ("zl", "yh", "yl", "x", "fz", "fc")
    )
    placed = (
        P(REP, FSDP, None),
        P(REP, FSDP, None),
        P(REP, FSDP, None),
        P(REP, FSDP, None),
        P(FSDP, REP),
        P(FSDP, REP),
    )
    return jax.shard_map(
        body,
        mesh=fine,
        in_specs=placed,
        out_specs=(
            P(FSDP, None),
            P(FSDP, REP),
            P(REP, FSDP, None),
            P(REP, FSDP, None),
        ),
        check_vma=False,
    )
```

```python
import math

import jax
import jax.numpy as jnp
from jax import lax
from jax.experimental import pallas as pl
from jax.experimental.pallas import tpu as pltpu
from jax.sharding import Mesh
from jax.sharding import PartitionSpec as P

beta_one = 0.9
beta_two = 0.95
inner_rate = 0.01
weight_decay = 0.1
adam_eps = 1e-08
clip_rms = 0.5
outer_rate = 0.7
outer_beta = 0.9

FSDP = ("fz", "fc")
NEAR = ("zl", "x", "yl")
FAR = ("yh",)
REP = ("zl", "yh", "yl", "x")

gain = outer_rate * (1.0 + outer_beta)
keep = 1.0 - gain
drag = outer_rate * outer_beta * outer_beta

SUB, LANE = 8, 128
PIECES = 4
SMALL = pltpu.CompilerParams(vmem_limit_bytes=4 * 2**20)
VMEM = pl.BlockSpec(memory_space=pltpu.VMEM)
ANY = pl.BlockSpec(memory_space=pl.ANY)
f32 = jnp.float32


def exchange(value, axes):
    return lax.all_to_all(value, axes, 0, 0, tiled=True)


def in_hbm(value):
    return pltpu.with_memory_space_constraint(value, pltpu.HBM)


def first_column(columns):
    index = 0
    for axis in REP:
        index = index * lax.axis_size(axis) + lax.axis_index(axis)
    return index * columns


def window(first, width):
    tile = jnp.minimum(first // LANE, width // LANE - 2)
    start = pl.multiple_of(tile * LANE, LANE)
    return start, first - start


def load_kernel(
    scale, grads_ref, weights_ref, first_ref, second_ref, anchor_ref, outer_ref,
    parts_ref, held_ref, base_ref, old_first_ref, old_second_ref, old_anchor_ref, old_outer_ref, arrived,
):
    rows, width = grads_ref.shape[1:]
    step = 2 * SUB
    cut = width // PIECES
    pieces = [(0, slice(top, top + step), slice(at, at + cut)) for top in range(0, rows, step) for at in range(0, width, cut)]
    count = 0

    def fetch(given, held):
        nonlocal count
        copy = pltpu.make_async_copy(given, held, arrived.at[count])
        copy.start()
        count += 1
        return copy

    grads = [fetch(grads_ref.at[here], held_ref.at[here]) for here in pieces]
    weights = [fetch(weights_ref.at[here], base_ref.at[here]) for here in pieces[::PIECES] for here in [here[:2]]]
    small = [fetch(anchor_ref, old_anchor_ref), fetch(outer_ref, old_outer_ref)]
    others = [
        fetch(given.at[here[:2]], held.at[here[:2]])
        for given, held in ((first_ref, old_first_ref), (second_ref, old_second_ref))
        for here in pieces[::PIECES]
    ]
    total = jnp.zeros((step, LANE), f32)
    for copy, (_, row, column) in zip(grads, pieces):
        copy.wait()
        for lane in range(column.start, column.stop, LANE):
            tile = held_ref[0, row, lane : lane + LANE].astype(f32)
            total += tile * tile
    tile = total[:SUB] + total[SUB:]
    parts_ref[...] = jnp.broadcast_to(tile[None], parts_ref.shape)
    for copy in small:
        copy.wait()
    mine = keep * old_anchor_ref[...] - drag * old_outer_ref[...]
    columns = mine.shape[1]
    start, shift = window(first_column(columns), width)
    mine = jnp.concatenate([mine, jnp.zeros((rows, 2 * LANE - columns), f32)], axis=1)
    mine = pltpu.roll(mine, shift, 1)
    for copy in weights:
        copy.wait()
    base_ref[...] = (scale * (1.0 - inner_rate * weight_decay)) * base_ref[...]
    base_ref[0, :, pl.ds(start, 2 * LANE)] += mine
    for copy in others:
        copy.wait()


def step_kernel(
    scale, entries, parts_ref, grads_ref, base_ref, old_first_ref, old_second_ref, blocks_ref, new_first_ref, new_second_ref
):
    rows, width = base_ref.shape[1:]
    cut = blocks_ref.shape[2]
    cuts = width // cut
    norm_square = jnp.sum(parts_ref[...])
    clip_factor = jnp.minimum(
        1.0, clip_rms * math.sqrt(entries) * lax.rsqrt(jnp.full((SUB, LANE), norm_square + 1e-06))
    )
    clip_row = clip_factor[:1, :1]
    for top in range(0, rows, 2 * SUB):
        for at in range(cuts):
            here = (0, slice(top, top + 2 * SUB), slice(at * cut, (at + 1) * cut))
            clipped = grads_ref[here].astype(f32) * clip_row
            new_first = beta_one * old_first_ref[here] + (1.0 - beta_one) * clipped
            new_second = beta_two * old_second_ref[here] + (1.0 - beta_two) * clipped * clipped
            new_first_ref[here] = new_first
            new_second_ref[here] = new_second
            block = base_ref[here] - (scale * inner_rate) * (new_first / (jnp.sqrt(new_second) + adam_eps))
            for half in range(2):
                blocks_ref[(top // SUB + half) * cuts + at] = block[half * SUB : (half + 1) * SUB]


def sum_kernel(given_ref, *refs):
    sums_ref = refs[-1]
    total = given_ref[0]
    for at in range(1, given_ref.shape[0]):
        total += given_ref[at]
    sums_ref[...] = jnp.broadcast_to(total[None], sums_ref.shape)


def sum_spread(given, n, *after):
    return pl.pallas_call(
        sum_kernel,
        out_shape=pltpu.VMEM((n,) + given.shape[1:], f32),
        in_specs=[VMEM] * (1 + len(after)),
        out_specs=VMEM,
        compiler_params=SMALL,
        name="sum",
    )(given, *after)


def copies_kernel(given_ref, *refs):
    out_ref, total_ref, done = refs[-3:]
    total = given_ref[0]
    for at in range(1, given_ref.shape[0]):
        total += given_ref[at]
    total_ref[...] = total
    copies = [pltpu.make_async_copy(total_ref, out_ref.at[at], done.at[at]) for at in range(out_ref.shape[0])]
    for copy in copies:
        copy.start()
    for copy in copies:
        copy.wait()


def sum_copies(given, n):
    return pl.pallas_call(
        copies_kernel,
        out_shape=jax.ShapeDtypeStruct((n,) + given.shape[1:], f32),
        in_specs=[VMEM],
        out_specs=ANY,
        scratch_shapes=[pltpu.VMEM(given.shape[1:], f32), pltpu.SemaphoreType.DMA((n,))],
        compiler_params=SMALL,
        name="copies",
    )(given)


def write_kernel(first_ref, second_ref, _after, new_first_ref, new_second_ref, mark_ref, done):
    copies = []
    for given, out in ((first_ref, new_first_ref), (second_ref, new_second_ref)):
        for at in range(0, given.shape[1], SUB):
            here = (0, slice(at, at + SUB))
            copies.append(pltpu.make_async_copy(given.at[here], out.at[here], done.at[len(copies)]))
            copies[-1].start()
    mark_ref[...] = jnp.zeros(mark_ref.shape, f32)
    for copy in copies:
        copy.wait()


def write_moments(first, second, after):
    return pl.pallas_call(
        write_kernel,
        out_shape=(jax.ShapeDtypeStruct(first.shape, f32),) * 2 + (pltpu.VMEM((SUB, LANE), f32),),
        in_specs=[VMEM, VMEM, ANY],
        out_specs=(ANY, ANY, VMEM),
        scratch_shapes=[pltpu.SemaphoreType.DMA((2 * first.shape[1] // SUB,))],
        compiler_params=SMALL,
        cost_estimate=pl.CostEstimate(flops=10**6, bytes_accessed=4 * 10**6, transcendentals=0),
        name="write",
    )(first, second, after)


def outer_kernel(
    full_ref, anchor_ref, outer_ref, first_ref, second_ref, params_ref, momentum_ref, new_first_ref, new_second_ref,
    own_ref, done,
):
    copies = []
    for given, out in ((first_ref, new_first_ref), (second_ref, new_second_ref)):
        for at in range(0, given.shape[1], SUB):
            here = (0, slice(at, at + SUB))
            copies.append(pltpu.make_async_copy(given.at[here], out.at[here], done.at[len(copies)]))
            copies[-1].start()
    for at in range(full_ref.shape[0] // SUB):
        here = slice(at * SUB, (at + 1) * SUB)
        copies.append(pltpu.make_async_copy(full_ref.at[here], params_ref.at[here], done.at[len(copies)]))
        copies[-1].start()
    columns = anchor_ref.shape[1]
    start, shift = window(first_column(columns), full_ref.shape[1])
    near = full_ref[:, pl.ds(start, 2 * LANE)]
    own = pltpu.roll(near, 2 * LANE - shift, 1)[:, :columns]
    mean = (own - keep * anchor_ref[...] + drag * outer_ref[...]) / gain
    own_ref[...] = outer_beta * outer_ref[...] + (anchor_ref[...] - mean)
    copies.append(pltpu.make_async_copy(own_ref, momentum_ref, done.at[len(copies)]))
    copies[-1].start()
    for copy in copies:
        copy.wait()


def body(inner_weights, grads, first_moment, second_moment, anchor, outer_momentum):
    rows, width = grads.shape[1:]
    shards = lax.axis_size(FSDP)
    replicas = lax.axis_size(REP)
    near = lax.axis_size(NEAR)
    far = lax.axis_size(FAR)
    columns = anchor.shape[1]
    groups = rows // SUB
    cuts = near // groups
    scale = gain / replicas

    def load(*refs):
        load_kernel(scale, *refs)

    given = (grads, inner_weights, first_moment, second_moment, anchor, outer_momentum)
    pieces = rows // (2 * SUB)
    parts, grads, base, old_first, old_second, anchor, outer_momentum = pl.pallas_call(
        load,
        out_shape=(pltpu.VMEM((shards, SUB, LANE), f32),) + tuple(pltpu.VMEM(a.shape, a.dtype) for a in given),
        in_specs=[ANY] * 6,
        out_specs=(VMEM,) * 7,
        scratch_shapes=[pltpu.SemaphoreType.DMA((pieces * (PIECES + 3) + 2,))],
        compiler_params=SMALL,
        name="load",
    )(*(in_hbm(a) for a in given))
    parts = exchange(parts, FSDP)

    def step(*refs):
        step_kernel(scale, rows * width * shards, *refs)

    blocks, new_first, new_second = pl.pallas_call(
        step,
        out_shape=(
            pltpu.VMEM((near, SUB, width // cuts), f32),
            pltpu.VMEM((1, rows, width), f32),
            pltpu.VMEM((1, rows, width), f32),
        ),
        in_specs=[VMEM] * 5,
        out_specs=(VMEM,) * 3,
        input_output_aliases={3: 1, 4: 2},
        compiler_params=SMALL,
        name="step",
    )(parts, grads, base, old_first, old_second)
    mine = sum_spread(exchange(blocks, NEAR), far)
    mine = sum_spread(exchange(mine, FAR), near)
    full = exchange(mine, NEAR)
    full = full.reshape(groups, cuts, SUB, width // cuts).transpose(0, 2, 1, 3).reshape(rows, width)
    new_params, new_momentum, new_first, new_second = pl.pallas_call(
        outer_kernel,
        out_shape=(jax.ShapeDtypeStruct((rows, width), f32), jax.ShapeDtypeStruct((rows, columns), f32))
        + (jax.ShapeDtypeStruct((1, rows, width), f32),) * 2,
        in_specs=[VMEM] * 5,
        out_specs=(ANY,) * 4,
        scratch_shapes=[pltpu.VMEM((rows, columns), f32), pltpu.SemaphoreType.DMA((3 * groups + 1,))],
        compiler_params=SMALL,
        name="outer",
    )(full, anchor, outer_momentum, new_first, new_second)
    return (new_params, new_momentum, new_first, new_second)


def solution(mesh):
    fine = Mesh(
        mesh.devices.reshape(2, 4, 2, 4, 4, 2), ("zl", "yh", "yl", "x", "fz", "fc")
    )
    placed = (
        P(REP, FSDP, None),
        P(REP, FSDP, None),
        P(REP, FSDP, None),
        P(REP, FSDP, None),
        P(FSDP, REP),
        P(FSDP, REP),
    )
    return jax.shard_map(
        body,
        mesh=fine,
        in_specs=placed,
        out_specs=(
            P(FSDP, None),
            P(FSDP, REP),
            P(REP, FSDP, None),
            P(REP, FSDP, None),
        ),
        check_vma=False,
    )
```

```python
import math

import jax
import jax.numpy as jnp
from jax import lax
from jax.experimental import pallas as pl
from jax.experimental.pallas import tpu as pltpu
from jax.sharding import Mesh
from jax.sharding import PartitionSpec as P

beta_one = 0.9
beta_two = 0.95
inner_rate = 0.01
weight_decay = 0.1
adam_eps = 1e-08
clip_rms = 0.5
outer_rate = 0.7
outer_beta = 0.9

FSDP = ("fz", "fc")
NEAR = ("zl", "x", "yl")
FAR = ("yh",)
REP = ("zl", "yh", "yl", "x")

gain = outer_rate * (1.0 + outer_beta)
keep = 1.0 - gain
drag = outer_rate * outer_beta * outer_beta

SUB, LANE = 8, 128
PIECES = 2
SHARES = 1
SMALL = pltpu.CompilerParams(vmem_limit_bytes=4 * 2**20)
VMEM = pl.BlockSpec(memory_space=pltpu.VMEM)
ANY = pl.BlockSpec(memory_space=pl.ANY)
f32 = jnp.float32


def exchange(value, axes):
    return lax.all_to_all(value, axes, 0, 0, tiled=True)


def in_hbm(value):
    return pltpu.with_memory_space_constraint(value, pltpu.HBM)


def first_column(columns):
    index = 0
    for axis in REP:
        index = index * lax.axis_size(axis) + lax.axis_index(axis)
    return index * columns


def window(first, width):
    tile = jnp.minimum(first // LANE, width // LANE - 2)
    start = pl.multiple_of(tile * LANE, LANE)
    return start, first - start


def load_kernel(grads_ref, *refs):
    *given, parts_ref, grads_held = refs[: len(refs) // 2 + 1]
    *held, arrived = refs[len(refs) // 2 + 1 :]
    rows, width = grads_ref.shape[1:]
    step = 2 * SUB
    cut = width // PIECES
    count = 0

    def fetch(source, target):
        nonlocal count
        copy = pltpu.make_async_copy(source, target, arrived.at[count])
        copy.start()
        count += 1
        return copy

    pieces = [(0, slice(top, top + step), slice(at, at + cut)) for top in range(0, rows, step) for at in range(0, width, cut)]
    grads = [fetch(grads_ref.at[here], grads_held.at[here]) for here in pieces]
    others = []
    for source, target in zip(given, held):
        if len(source.shape) == 3:
            size = rows // SHARES
            for top in range(0, rows, size):
                others.append(fetch(source.at[0, top : top + size], target.at[0, top : top + size]))
        else:
            others.append(fetch(source, target))
    total = jnp.zeros((step, LANE), f32)
    for copy, (_, row, column) in zip(grads, pieces):
        copy.wait()
        for lane in range(column.start, column.stop, LANE):
            tile = grads_held[0, row, lane : lane + LANE].astype(f32)
            total += tile * tile
    tile = total[:SUB] + total[SUB:]
    parts_ref[...] = jnp.broadcast_to(jnp.sum(tile, axis=0, keepdims=True), parts_ref.shape)
    for copy in others:
        copy.wait()


def step_kernel(
    scale, entries, parts_ref, grads_ref, weights_ref, first_ref, second_ref, anchor_ref, outer_ref,
    blocks_ref, new_first_ref, new_second_ref,
):
    rows, width = weights_ref.shape[1:]
    cut = blocks_ref.shape[2]
    cuts = width // cut
    norm_square = jnp.sum(parts_ref[...])
    clip_factor = jnp.minimum(
        1.0, clip_rms * math.sqrt(entries) * lax.rsqrt(jnp.full((SUB, LANE), norm_square + 1e-06))
    )
    clip_row = clip_factor[:1, :1]
    for top in range(0, rows, 2 * SUB):
        for at in range(cuts):
            here = (0, slice(top, top + 2 * SUB), slice(at * cut, (at + 1) * cut))
            clipped = grads_ref[here].astype(f32) * clip_row
            new_first = beta_one * first_ref[here] + (1.0 - beta_one) * clipped
            new_second = beta_two * second_ref[here] + (1.0 - beta_two) * clipped * clipped
            new_first_ref[here] = new_first
            new_second_ref[here] = new_second
            block = (scale * (1.0 - inner_rate * weight_decay)) * weights_ref[here]
            block -= (scale * inner_rate) * (new_first / (jnp.sqrt(new_second) + adam_eps))
            for half in range(2):
                blocks_ref[(top // SUB + half) * cuts + at] = block[half * SUB : (half + 1) * SUB]
    mine = keep * anchor_ref[...] - drag * outer_ref[...]
    columns = mine.shape[1]
    first = first_column(columns)
    block = first // cut
    start, shift = window(first - block * cut, cut)
    mine = jnp.concatenate([mine, jnp.zeros((rows, 2 * LANE - columns), f32)], axis=1)
    mine = pltpu.roll(mine, shift, 1)
    for group in range(rows // SUB):
        blocks_ref[group * cuts + block, :, pl.ds(start, 2 * LANE)] += mine[group * SUB : (group + 1) * SUB]


def sum_kernel(given_ref, *refs):
    sums_ref = refs[-1]
    total = given_ref[0]
    for at in range(1, given_ref.shape[0]):
        total += given_ref[at]
    sums_ref[...] = jnp.broadcast_to(total[None], sums_ref.shape)


def sum_spread(given, n, *after):
    return pl.pallas_call(
        sum_kernel,
        out_shape=pltpu.VMEM((n,) + given.shape[1:], f32),
        in_specs=[VMEM] * (1 + len(after)),
        out_specs=VMEM,
        compiler_params=SMALL,
        name="sum",
    )(given, *after)


def copies_kernel(given_ref, *refs):
    out_ref, total_ref, done = refs[-3:]
    total = given_ref[0]
    for at in range(1, given_ref.shape[0]):
        total += given_ref[at]
    total_ref[...] = total
    copies = [pltpu.make_async_copy(total_ref, out_ref.at[at], done.at[at]) for at in range(out_ref.shape[0])]
    for copy in copies:
        copy.start()
    for copy in copies:
        copy.wait()


def sum_copies(given, n):
    return pl.pallas_call(
        copies_kernel,
        out_shape=jax.ShapeDtypeStruct((n,) + given.shape[1:], f32),
        in_specs=[VMEM],
        out_specs=ANY,
        scratch_shapes=[pltpu.VMEM(given.shape[1:], f32), pltpu.SemaphoreType.DMA((n,))],
        compiler_params=SMALL,
        name="copies",
    )(given)


def write_kernel(first_ref, second_ref, _after, new_first_ref, new_second_ref, mark_ref, done):
    copies = []
    for given, out in ((first_ref, new_first_ref), (second_ref, new_second_ref)):
        for at in range(0, given.shape[1], 2 * SUB):
            here = (0, slice(at, at + 2 * SUB))
            copies.append(pltpu.make_async_copy(given.at[here], out.at[here], done.at[len(copies)]))
            copies[-1].start()
    mark_ref[...] = jnp.zeros(mark_ref.shape, f32)
    for copy in copies:
        copy.wait()


def write_moments(first, second, after):
    return pl.pallas_call(
        write_kernel,
        out_shape=(jax.ShapeDtypeStruct(first.shape, f32),) * 2 + (pltpu.VMEM((SUB, LANE), f32),),
        in_specs=[VMEM, VMEM, ANY],
        out_specs=(ANY, ANY, VMEM),
        scratch_shapes=[pltpu.SemaphoreType.DMA((2 * first.shape[1] // SUB,))],
        compiler_params=SMALL,
        cost_estimate=pl.CostEstimate(flops=10**6, bytes_accessed=4 * 10**6, transcendentals=0),
        name="write",
    )(first, second, after)


def outer_kernel(
    full_ref, anchor_ref, outer_ref, first_ref, second_ref, params_ref, momentum_ref, new_first_ref, new_second_ref,
    own_ref, done,
):
    copies = []
    for given, out in ((first_ref, new_first_ref), (second_ref, new_second_ref)):
        for at in range(0, given.shape[1], 2 * SUB):
            here = (0, slice(at, at + 2 * SUB))
            copies.append(pltpu.make_async_copy(given.at[here], out.at[here], done.at[len(copies)]))
            copies[-1].start()
    for at in range(full_ref.shape[0] // SUB):
        here = slice(at * SUB, (at + 1) * SUB)
        copies.append(pltpu.make_async_copy(full_ref.at[here], params_ref.at[here], done.at[len(copies)]))
        copies[-1].start()
    columns = anchor_ref.shape[1]
    start, shift = window(first_column(columns), full_ref.shape[1])
    near = full_ref[:, pl.ds(start, 2 * LANE)]
    own = pltpu.roll(near, 2 * LANE - shift, 1)[:, :columns]
    mean = (own - keep * anchor_ref[...] + drag * outer_ref[...]) / gain
    own_ref[...] = outer_beta * outer_ref[...] + (anchor_ref[...] - mean)
    copies.append(pltpu.make_async_copy(own_ref, momentum_ref, done.at[len(copies)]))
    copies[-1].start()
    for copy in copies:
        copy.wait()


def body(inner_weights, grads, first_moment, second_moment, anchor, outer_momentum):
    rows, width = grads.shape[1:]
    shards = lax.axis_size(FSDP)
    replicas = lax.axis_size(REP)
    near = lax.axis_size(NEAR)
    far = lax.axis_size(FAR)
    columns = anchor.shape[1]
    groups = rows // SUB
    cuts = near // groups
    scale = gain / replicas

    given = (grads, inner_weights, first_moment, second_moment, anchor, outer_momentum)
    pieces = rows // (2 * SUB)
    parts, *given = pl.pallas_call(
        load_kernel,
        out_shape=(pltpu.VMEM((shards, LANE), f32),) + tuple(pltpu.VMEM(a.shape, a.dtype) for a in given),
        in_specs=[ANY] * 6,
        out_specs=(VMEM,) * 7,
        scratch_shapes=[pltpu.SemaphoreType.DMA((pieces * PIECES + 3 * SHARES + 2,))],
        compiler_params=SMALL,
        name="load",
    )(*(in_hbm(a) for a in given))
    grads, inner_weights, first_moment, second_moment, anchor, outer_momentum = given
    parts = exchange(parts, FSDP)

    def step(*refs):
        step_kernel(scale, rows * width * shards, *refs)

    blocks, new_first, new_second = pl.pallas_call(
        step,
        out_shape=(
            pltpu.VMEM((near, SUB, width // cuts), f32),
            pltpu.VMEM((1, rows, width), f32),
            pltpu.VMEM((1, rows, width), f32),
        ),
        in_specs=[VMEM] * 7,
        out_specs=(VMEM,) * 3,
        input_output_aliases={3: 1, 4: 2},
        compiler_params=SMALL,
        name="step",
    )(parts, grads, inner_weights, first_moment, second_moment, anchor, outer_momentum)
    mine = sum_spread(exchange(blocks, NEAR), far)
    mine = sum_spread(exchange(mine, FAR), near)
    full = exchange(mine, NEAR)
    full = full.reshape(groups, cuts, SUB, width // cuts).transpose(0, 2, 1, 3).reshape(rows, width)
    new_params, new_momentum, new_first, new_second = pl.pallas_call(
        outer_kernel,
        out_shape=(jax.ShapeDtypeStruct((rows, width), f32), jax.ShapeDtypeStruct((rows, columns), f32))
        + (jax.ShapeDtypeStruct((1, rows, width), f32),) * 2,
        in_specs=[VMEM] * 5,
        out_specs=(ANY,) * 4,
        scratch_shapes=[pltpu.VMEM((rows, columns), f32), pltpu.SemaphoreType.DMA((3 * groups + 1,))],
        compiler_params=SMALL,
        name="outer",
    )(full, anchor, outer_momentum, new_first, new_second)
    return (new_params, new_momentum, new_first, new_second)


def solution(mesh):
    fine = Mesh(
        mesh.devices.reshape(2, 4, 2, 4, 4, 2), ("zl", "yh", "yl", "x", "fz", "fc")
    )
    placed = (
        P(REP, FSDP, None),
        P(REP, FSDP, None),
        P(REP, FSDP, None),
        P(REP, FSDP, None),
        P(FSDP, REP),
        P(FSDP, REP),
    )
    return jax.shard_map(
        body,
        mesh=fine,
        in_specs=placed,
        out_specs=(
            P(FSDP, None),
            P(FSDP, REP),
            P(REP, FSDP, None),
            P(REP, FSDP, None),
        ),
        check_vma=False,
    )
```

```python
import math

import jax
import jax.numpy as jnp
from jax import lax
from jax.experimental import pallas as pl
from jax.experimental.pallas import tpu as pltpu
from jax.sharding import Mesh
from jax.sharding import PartitionSpec as P

beta_one = 0.9
beta_two = 0.95
inner_rate = 0.01
weight_decay = 0.1
adam_eps = 1e-08
clip_rms = 0.5
outer_rate = 0.7
outer_beta = 0.9

FSDP = ("fz", "fc")
NEAR = ("zl", "x", "yl")
FAR = ("yh",)
REP = ("zl", "yh", "yl", "x")

gain = outer_rate * (1.0 + outer_beta)
keep = 1.0 - gain
drag = outer_rate * outer_beta * outer_beta

SUB, LANE = 8, 128
PIECES = 2
SHARES = 1
SMALL = pltpu.CompilerParams(vmem_limit_bytes=4 * 2**20)
VMEM = pl.BlockSpec(memory_space=pltpu.VMEM)
ANY = pl.BlockSpec(memory_space=pl.ANY)
f32 = jnp.float32


def exchange(value, axes):
    return lax.all_to_all(value, axes, 0, 0, tiled=True)


def in_hbm(value):
    return pltpu.with_memory_space_constraint(value, pltpu.HBM)


def first_column(columns):
    index = 0
    for axis in REP:
        index = index * lax.axis_size(axis) + lax.axis_index(axis)
    return index * columns


def window(first, width):
    tile = jnp.minimum(first // LANE, width // LANE - 2)
    start = pl.multiple_of(tile * LANE, LANE)
    return start, first - start


def load_kernel(grads_ref, *refs):
    *given, parts_ref, grads_held = refs[: len(refs) // 2 + 1]
    *held, arrived = refs[len(refs) // 2 + 1 :]
    rows, width = grads_ref.shape[1:]
    step = 2 * SUB
    cut = width // PIECES
    count = 0

    def fetch(source, target):
        nonlocal count
        copy = pltpu.make_async_copy(source, target, arrived.at[count])
        copy.start()
        count += 1
        return copy

    pieces = [(0, slice(top, top + step), slice(at, at + cut)) for top in range(0, rows, step) for at in range(0, width, cut)]
    grads = [fetch(grads_ref.at[here], grads_held.at[here]) for here in pieces]
    others = []
    for source, target in zip(given, held):
        if len(source.shape) == 3:
            size = rows // SHARES
            for top in range(0, rows, size):
                others.append(fetch(source.at[0, top : top + size], target.at[0, top : top + size]))
        else:
            others.append(fetch(source, target))
    total = jnp.zeros((step, LANE), f32)
    for copy, (_, row, column) in zip(grads, pieces):
        copy.wait()
        for lane in range(column.start, column.stop, LANE):
            tile = grads_held[0, row, lane : lane + LANE].astype(f32)
            total += tile * tile
    tile = total[:SUB] + total[SUB:]
    parts_ref[...] = jnp.broadcast_to(jnp.sum(tile, axis=0, keepdims=True), parts_ref.shape)
    for copy in others:
        copy.wait()


def step_kernel(
    scale, entries, parts_ref, grads_ref, weights_ref, first_ref, second_ref, anchor_ref, outer_ref,
    blocks_ref, new_first_ref, new_second_ref,
):
    rows, width = weights_ref.shape[1:]
    cut = blocks_ref.shape[2]
    cuts = width // cut
    norm_square = jnp.sum(parts_ref[...])
    clip_factor = jnp.minimum(
        1.0, clip_rms * math.sqrt(entries) * lax.rsqrt(jnp.full((SUB, LANE), norm_square + 1e-06))
    )
    clip_row = clip_factor[:1, :1]
    for top in range(0, rows, 2 * SUB):
        for at in range(cuts):
            here = (0, slice(top, top + 2 * SUB), slice(at * cut, (at + 1) * cut))
            clipped = grads_ref[here].astype(f32) * clip_row
            new_first = beta_one * first_ref[here] + (1.0 - beta_one) * clipped
            new_second = beta_two * second_ref[here] + (1.0 - beta_two) * clipped * clipped
            new_first_ref[here] = new_first
            new_second_ref[here] = new_second
            block = (scale * (1.0 - inner_rate * weight_decay)) * weights_ref[here]
            block -= (scale * inner_rate) * (new_first / (new_second * lax.rsqrt(new_second) + adam_eps))
            for half in range(2):
                blocks_ref[(top // SUB + half) * cuts + at] = block[half * SUB : (half + 1) * SUB]
    mine = keep * anchor_ref[...] - drag * outer_ref[...]
    columns = mine.shape[1]
    first = first_column(columns)
    block = first // cut
    start, shift = window(first - block * cut, cut)
    mine = jnp.concatenate([mine, jnp.zeros((rows, 2 * LANE - columns), f32)], axis=1)
    mine = pltpu.roll(mine, shift, 1)
    for group in range(rows // SUB):
        blocks_ref[group * cuts + block, :, pl.ds(start, 2 * LANE)] += mine[group * SUB : (group + 1) * SUB]


def sum_kernel(given_ref, *refs):
    sums_ref = refs[-1]
    total = given_ref[0]
    for at in range(1, given_ref.shape[0]):
        total += given_ref[at]
    sums_ref[...] = jnp.broadcast_to(total[None], sums_ref.shape)


def sum_spread(given, n, *after):
    return pl.pallas_call(
        sum_kernel,
        out_shape=pltpu.VMEM((n,) + given.shape[1:], f32),
        in_specs=[VMEM] * (1 + len(after)),
        out_specs=VMEM,
        compiler_params=SMALL,
        name="sum",
    )(given, *after)


def copies_kernel(given_ref, *refs):
    out_ref, total_ref, done = refs[-3:]
    total = given_ref[0]
    for at in range(1, given_ref.shape[0]):
        total += given_ref[at]
    total_ref[...] = total
    copies = [pltpu.make_async_copy(total_ref, out_ref.at[at], done.at[at]) for at in range(out_ref.shape[0])]
    for copy in copies:
        copy.start()
    for copy in copies:
        copy.wait()


def sum_copies(given, n):
    return pl.pallas_call(
        copies_kernel,
        out_shape=jax.ShapeDtypeStruct((n,) + given.shape[1:], f32),
        in_specs=[VMEM],
        out_specs=ANY,
        scratch_shapes=[pltpu.VMEM(given.shape[1:], f32), pltpu.SemaphoreType.DMA((n,))],
        compiler_params=SMALL,
        name="copies",
    )(given)


def write_kernel(first_ref, second_ref, _after, new_first_ref, new_second_ref, mark_ref, done):
    copies = []
    for given, out in ((first_ref, new_first_ref), (second_ref, new_second_ref)):
        for at in range(0, given.shape[1], 2 * SUB):
            here = (0, slice(at, at + 2 * SUB))
            copies.append(pltpu.make_async_copy(given.at[here], out.at[here], done.at[len(copies)]))
            copies[-1].start()
    mark_ref[...] = jnp.zeros(mark_ref.shape, f32)
    for copy in copies:
        copy.wait()


def write_moments(first, second, after):
    return pl.pallas_call(
        write_kernel,
        out_shape=(jax.ShapeDtypeStruct(first.shape, f32),) * 2 + (pltpu.VMEM((SUB, LANE), f32),),
        in_specs=[VMEM, VMEM, ANY],
        out_specs=(ANY, ANY, VMEM),
        scratch_shapes=[pltpu.SemaphoreType.DMA((2 * first.shape[1] // SUB,))],
        compiler_params=SMALL,
        cost_estimate=pl.CostEstimate(flops=10**6, bytes_accessed=4 * 10**6, transcendentals=0),
        name="write",
    )(first, second, after)


def outer_kernel(
    full_ref, anchor_ref, outer_ref, first_ref, second_ref, params_ref, momentum_ref, new_first_ref, new_second_ref,
    own_ref, done,
):
    copies = []
    for given, out in ((first_ref, new_first_ref), (second_ref, new_second_ref)):
        for at in range(0, given.shape[1], 2 * SUB):
            here = (0, slice(at, at + 2 * SUB))
            copies.append(pltpu.make_async_copy(given.at[here], out.at[here], done.at[len(copies)]))
            copies[-1].start()
    for at in range(full_ref.shape[0] // SUB):
        here = slice(at * SUB, (at + 1) * SUB)
        copies.append(pltpu.make_async_copy(full_ref.at[here], params_ref.at[here], done.at[len(copies)]))
        copies[-1].start()
    columns = anchor_ref.shape[1]
    start, shift = window(first_column(columns), full_ref.shape[1])
    near = full_ref[:, pl.ds(start, 2 * LANE)]
    own = pltpu.roll(near, 2 * LANE - shift, 1)[:, :columns]
    mean = (own - keep * anchor_ref[...] + drag * outer_ref[...]) / gain
    own_ref[...] = outer_beta * outer_ref[...] + (anchor_ref[...] - mean)
    copies.append(pltpu.make_async_copy(own_ref, momentum_ref, done.at[len(copies)]))
    copies[-1].start()
    for copy in copies:
        copy.wait()


def body(inner_weights, grads, first_moment, second_moment, anchor, outer_momentum):
    rows, width = grads.shape[1:]
    shards = lax.axis_size(FSDP)
    replicas = lax.axis_size(REP)
    near = lax.axis_size(NEAR)
    far = lax.axis_size(FAR)
    columns = anchor.shape[1]
    groups = rows // SUB
    cuts = near // groups
    scale = gain / replicas

    given = (grads, inner_weights, first_moment, second_moment)
    pieces = rows // (2 * SUB)
    parts, *given = pl.pallas_call(
        load_kernel,
        out_shape=(pltpu.VMEM((shards, LANE), f32),) + tuple(pltpu.VMEM(a.shape, a.dtype) for a in given),
        in_specs=[ANY] * 4,
        out_specs=(VMEM,) * 5,
        scratch_shapes=[pltpu.SemaphoreType.DMA((pieces * PIECES + 3 * SHARES,))],
        compiler_params=SMALL,
        name="load",
    )(*(in_hbm(a) for a in given))
    grads, inner_weights, first_moment, second_moment = given
    parts = exchange(parts, FSDP)

    def step(*refs):
        step_kernel(scale, rows * width * shards, *refs)

    blocks, new_first, new_second = pl.pallas_call(
        step,
        out_shape=(
            pltpu.VMEM((near, SUB, width // cuts), f32),
            pltpu.VMEM((1, rows, width), f32),
            pltpu.VMEM((1, rows, width), f32),
        ),
        in_specs=[VMEM] * 7,
        out_specs=(VMEM,) * 3,
        input_output_aliases={3: 1, 4: 2},
        compiler_params=SMALL,
        name="step",
    )(parts, grads, inner_weights, first_moment, second_moment, anchor, outer_momentum)
    mine = sum_spread(exchange(blocks, NEAR), far)
    mine = sum_spread(exchange(mine, FAR), near)
    full = exchange(mine, NEAR)
    full = full.reshape(groups, cuts, SUB, width // cuts).transpose(0, 2, 1, 3).reshape(rows, width)
    new_params, new_momentum, new_first, new_second = pl.pallas_call(
        outer_kernel,
        out_shape=(jax.ShapeDtypeStruct((rows, width), f32), jax.ShapeDtypeStruct((rows, columns), f32))
        + (jax.ShapeDtypeStruct((1, rows, width), f32),) * 2,
        in_specs=[VMEM] * 5,
        out_specs=(ANY,) * 4,
        scratch_shapes=[pltpu.VMEM((rows, columns), f32), pltpu.SemaphoreType.DMA((3 * groups + 1,))],
        compiler_params=SMALL,
        name="outer",
    )(full, anchor, outer_momentum, new_first, new_second)
    return (new_params, new_momentum, new_first, new_second)


def solution(mesh):
    fine = Mesh(
        mesh.devices.reshape(2, 4, 2, 4, 4, 2), ("zl", "yh", "yl", "x", "fz", "fc")
    )
    placed = (
        P(REP, FSDP, None),
        P(REP, FSDP, None),
        P(REP, FSDP, None),
        P(REP, FSDP, None),
        P(FSDP, REP),
        P(FSDP, REP),
    )
    return jax.shard_map(
        body,
        mesh=fine,
        in_specs=placed,
        out_specs=(
            P(FSDP, None),
            P(FSDP, REP),
            P(REP, FSDP, None),
            P(REP, FSDP, None),
        ),
        check_vma=False,
    )
```
